512 devices in a mesh: blk: 16 (over z), uly: 8 (over x, y_hi), clip: 4 (over y_lo, core).
Axes of the slice: x: 4, y: 4 (y_hi: 2, y_lo: 2; y = y_hi * 2 + y_lo), z: 16, core: 2. Of those that a mesh axis runs over, the one named last changes fastest.
Arguments:
- self_queries: bfloat16 [16384, 3072], P(('clip', 'blk', 'uly')), parts along dimension 0, may hold values from -160 to 160
- self_keys: bfloat16 [16384, 3072], P(('clip', 'blk', 'uly')), parts along dimension 0, may hold values from -6 to 6
- self_values: bfloat16 [16384, 3072], P(('clip', 'blk', 'uly')), parts along dimension 0, may hold values from -6 to 6
- cross_queries: bfloat16 [16384, 3072], P(('clip', 'blk', 'uly')), parts along dimension 0, may hold values from -160 to 160
- text_rows: bfloat16 [1024, 4096], P('clip'), parts along dimension 0, may hold values from -6 to 6
- text_projection: bfloat16 [4096, 2, 3072], P('blk', None, 'uly'), may hold values from -0.09375 to 0.09375
Outputs:
- attended: bfloat16 [16384, 3072], P(('clip', 'blk', 'uly')), parts along dimension 0
The draws below stay inside these ranges and needn't reach their ends.
There are 4 independent parts, one for each index of `clip`. The reference program is written for one: setup_inputs(seed, part) draws one part's arguments, and reference() takes and returns one part's arrays. A program takes and returns all parts, laid end to end along the dimension named above; an argument that names none is the same for every part. Nothing has to cross between parts.
All inputs are finite; a program needn't handle non-finite values.
Results may differ from the reference program's by a relative error of at most 0.012.
Values may be sent and summed in bfloat16 or wider, within the bound.
A program may use at most 128 MiB of HBM per device.

```python
import jax
import jax.numpy as jnp
from jax import lax

HEADS = 24
HEAD_DIM = 128
TEXT_WIDTH = 4096
TEXT_ROWS = 256
TOKENS = 4096


def scaled_rows(key, base_scale):
    first = jax.random.fold_in(key, 0)
    shape = (TOKENS, HEADS * HEAD_DIM)
    return jnp.clip(base_scale * jax.random.normal(first, shape, jnp.float32), -15.0, 15.0)


def draw_self_queries(key, part):
    key = jax.random.fold_in(key, 11)
    return scaled_rows(key, 2.5).astype(jnp.bfloat16)


def draw_cross_queries(key, part):
    key = jax.random.fold_in(key, 23)
    return scaled_rows(key, 2.5).astype(jnp.bfloat16)


def block_levels(key, dims, shards, low, high):
    loudness, own = 1.0, jax.random.fold_in(key, 6)
    for dim, blocks in shards:
        steps = jnp.exp(jax.random.uniform(jax.random.fold_in(own, dim), (blocks,), jnp.float32, low / len(shards), high / len(shards)))
        loudness = loudness * jnp.repeat(steps, dims[dim] // blocks).reshape([-1 if axis == dim else 1 for axis in range(len(dims))])
    return loudness


def noise(stream_key, extent, spread, most, pieces=(), held_as=jnp.bfloat16):
    values = spread * jax.random.normal(stream_key, extent, jnp.float32)
    if pieces:
        values = values * block_levels(stream_key, extent, pieces, -0.22, 0.18)
    return jnp.clip(values, -most, most).astype(held_as)


def setup_inputs(seed: int = 0, part: int = 0) -> dict:
    key_of = jax.random.split(jax.random.key(seed), 7)
    part_keys = jax.random.split(jax.random.fold_in(key_of[6], part), 7)
    self_queries = draw_self_queries(jax.random.fold_in(jax.random.fold_in(key_of[6], part), 71), part)
    self_keys = noise(part_keys[1], (TOKENS, HEADS * HEAD_DIM), 1.0, 6.0, ((0, 128),))
    self_values = noise(part_keys[2], (TOKENS, HEADS * HEAD_DIM), 1.0, 6.0, ((0, 128),))
    cross_queries = draw_cross_queries(jax.random.fold_in(jax.random.fold_in(key_of[6], part), 71), part)
    text_rows = noise(part_keys[4], (TEXT_ROWS, TEXT_WIDTH), 1.0, 6.0)
    text_projection = noise(key_of[5], (TEXT_WIDTH, 2, HEADS * HEAD_DIM), TEXT_WIDTH ** -0.5, 0.09375, ((0, 16), (2, 8)))
    return dict(self_queries=self_queries, self_keys=self_keys, self_values=self_values, cross_queries=cross_queries, text_rows=text_rows, text_projection=text_projection)


def soft_attend(query_rows, key_rows, value_rows, score_scale):
    scores = jnp.dot(query_rows, key_rows.T, preferred_element_type=jnp.float32) * score_scale
    row_top = jnp.max(scores, axis=-1, keepdims=True)
    weights = jnp.exp(scores - row_top)
    row_total = jnp.sum(weights, axis=-1, keepdims=True)
    blended = jnp.dot(weights.astype(jnp.bfloat16), value_rows, preferred_element_type=jnp.float32)
    return blended / row_total


def reference(self_queries, self_keys, self_values, cross_queries, text_rows, text_projection):
    score_scale = HEAD_DIM ** -0.5
    token_count = self_queries.shape[0]

    def head_major(array):
        return array.reshape(array.shape[0], HEADS, HEAD_DIM).transpose(1, 0, 2)

    flat_weight = text_projection.reshape(TEXT_WIDTH, 2 * HEADS * HEAD_DIM)
    text_kv = jnp.dot(text_rows, flat_weight, preferred_element_type=jnp.float32).astype(jnp.bfloat16)
    text_kv = text_kv.reshape(TEXT_ROWS, 2, HEADS * HEAD_DIM)
    text_keys = head_major(text_kv[:, 0])
    text_vals = head_major(text_kv[:, 1])

    def one_head(operands):
        query_head, key_head, value_head, cross_head, tkey_head, tval_head = operands

        def one_block(block_pair):
            self_part = soft_attend(block_pair[0], key_head, value_head, score_scale)
            cross_part = soft_attend(block_pair[1], tkey_head, tval_head, score_scale)
            return self_part + cross_part

        query_blocks = query_head.reshape(8, token_count // 8, HEAD_DIM)
        cross_blocks = cross_head.reshape(8, token_count // 8, HEAD_DIM)
        summed = lax.map(one_block, (query_blocks, cross_blocks))
        return summed.reshape(token_count, HEAD_DIM)

    outputs = lax.map(one_head, (head_major(self_queries), head_major(self_keys), head_major(self_values),
                                 head_major(cross_queries), text_keys, text_vals))
    return outputs.transpose(1, 0, 2).reshape(token_count, HEADS * HEAD_DIM).astype(jnp.bfloat16)
```

```python
import math

import jax
import jax.numpy as jnp
from jax import lax
from jax.experimental import pallas as pl
from jax.experimental.pallas import tpu as pltpu
from jax.sharding import PartitionSpec as P

HEADS = 24
HEAD_DIM = 128
NX, NY, NZ = 4, 2, 16
SOURCES = NY * NZ
GROUPS = NX * NY
ROWS = 32
HALF = ROWS // 2
GROUP_COLS = HEADS // GROUPS * HEAD_DIM
TEXT_ROWS = 256
CHUNK = TEXT_ROWS // NZ
FEATURES = 256
TILE = 256
TILE_SOURCES = TILE // HALF
EXP_SCALE = math.log2(math.e) / math.sqrt(HEAD_DIM)
F32, BF16 = jnp.float32, jnp.bfloat16


def remote(src, dst, send_sem, recv_sem, device):
    return pltpu.make_async_remote_copy(
        src_ref=src,
        dst_ref=dst,
        send_sem=send_sem,
        recv_sem=recv_sem,
        device_id=device,
        device_id_type=pl.DeviceIdType.MESH,
    )


def drain(ref, sem):
    pltpu.make_async_copy(ref, ref, sem).wait()


def slot_of(head):
    pair, place = head // 3, head % 3
    z = 2 * pair + jnp.where(place == 2, 1, 0)
    y = jnp.where(place == 2, pair % 2, place)
    return z, y


def scores_of(queries, keys):
    return lax.dot_general(queries, keys, (((1,), (1,)), ((), ())), preferred_element_type=F32)


def attend(queries, blocks):
    top = total = acc = None
    for keys, values in blocks:
        scores = scores_of(queries, keys())
        block_top = jnp.max(scores, axis=1, keepdims=True)
        new_top = block_top if top is None else jnp.maximum(top, block_top)
        weights = jnp.exp2((scores - new_top) * EXP_SCALE)
        block_total = jnp.sum(weights, axis=1, keepdims=True)
        update = jnp.dot(weights.astype(BF16), values(), preferred_element_type=F32)
        if top is None:
            total, acc = block_total, update
        else:
            shrink = jnp.exp2((top - new_top) * EXP_SCALE)
            total = total * shrink + block_total
            acc = acc * shrink + update
        top = new_top
    return acc / total


def kernel(
    q_hbm, k_hbm, v_hbm, cq_hbm, text_hbm, proj_hbm, out_ref,
    q_in, k_in, v_in, cq_in, text_in, proj_in,
    kv_stage, kv, q_got, o_stage, o_got,
    cq_got, co_stage, co_got,
    part, up_got, down_got, text_kv,
    load_sem, kv_send, kv_recv, q_send, q_recv, x_send, x_recv, cross_send, cross_recv,
    rs_send, rs_recv, ag_send, ag_recv, o_send, o_recv,
):
    z, uly, clip = lax.axis_index("blk"), lax.axis_index("uly"), lax.axis_index("clip")
    x, y = uly // NY, uly % NY
    me = z * NY + y
    active = jnp.logical_or(z % 2 == 0, y == (z // 2) % 2)
    my_head = 3 * (z // 2) + jnp.where(z % 2 == 0, y, 2)
    first_head = 3 * (z // 2) + 2 * (z % 2)

    def device(to_z, to_x, to_y):
        return (to_z, to_x * NY + to_y, clip)

    barrier = pltpu.get_barrier_semaphore()

    @pl.loop(1, SOURCES)
    def _(k):
        s = lax.rem(me + k, SOURCES)
        pl.semaphore_signal(
            barrier, inc=1, device_id=device(s // NY, x, s % NY), device_id_type=pl.DeviceIdType.MESH
        )

    @pl.loop(0, NY * (NX - 1))
    def _(k):
        to_x = lax.rem(x + 1 + k // NY, NX)
        pl.semaphore_signal(
            barrier, inc=1, device_id=device(z, to_x, k % NY), device_id_type=pl.DeviceIdType.MESH
        )

    loads = [
        pltpu.make_async_copy(k_hbm, k_in, load_sem.at[0]),
        pltpu.make_async_copy(v_hbm, v_in, load_sem.at[1]),
        pltpu.make_async_copy(
            text_hbm.at[:, pl.ds(pl.multiple_of(z * FEATURES, FEATURES), FEATURES)], text_in, load_sem.at[2]
        ),
        pltpu.make_async_copy(proj_hbm, proj_in, load_sem.at[3]),
        pltpu.make_async_copy(cq_hbm, cq_in, load_sem.at[4]),
        pltpu.make_async_copy(q_hbm, q_in, load_sem.at[5]),
    ]
    for load in loads:
        load.start()
    loads[0].wait()
    loads[1].wait()
    for h in range(HEADS):
        cols = slice(h * HEAD_DIM, (h + 1) * HEAD_DIM)
        for g in range(2):
            rows = slice(g * HALF, (g + 1) * HALF)
            kv_stage[g, h, 0] = k_in[rows, cols]
            kv_stage[g, h, 1] = v_in[rows, cols]
    loads[2].wait()
    loads[3].wait()
    part[...] = jnp.dot(text_in[...], proj_in[...], preferred_element_type=F32).reshape(part.shape)
    loads[4].wait()
    loads[5].wait()

    pl.semaphore_wait(barrier, SOURCES - 1 + NY * (NX - 1))

    def send_heads(source, target, send_sem, recv_sem):
        @pl.loop(0, HEADS)
        def _(k):
            h = lax.rem(first_head + k, HEADS)
            to_z, to_y = slot_of(h)
            mine = jnp.logical_and(to_z == z, to_y == y)

            @pl.when(mine)
            def _():
                pltpu.make_async_copy(source(h), target, recv_sem).start()

            @pl.when(jnp.logical_not(mine))
            def _():
                remote(source(h), target, send_sem, recv_sem, device(to_z, x, to_y)).start()

    def send_kv(g):
        send_heads(lambda h: kv_stage.at[g, h], kv.at[x, g, me], kv_send.at[g], kv_recv.at[g])

    def send_q(g):
        def source(h):
            return q_in.at[pl.ds(g * HALF, HALF), pl.ds(pl.multiple_of(h * HEAD_DIM, HEAD_DIM), HEAD_DIM)]

        send_heads(source, q_got.at[g, me], q_send.at[g], q_recv.at[g])

    def to_groups(source, target, send_sem, recv_sem):
        @pl.loop(1, GROUPS)
        def _(k):
            to = lax.rem(uly + k, GROUPS)
            remote(source(to), target, send_sem, recv_sem, device(z, to // NY, to % NY)).start()

        pltpu.make_async_copy(source(uly), target, recv_sem).start()

    def x_copy(g, j):
        step = (1, 3, 2)[j]
        return remote(
            kv.at[x, g], kv.at[x, g], x_send.at[g, j], x_recv.at[g, j], device(z, lax.rem(x + step, NX), y)
        )

    def gather_x(g):
        @pl.when(active)
        def _():
            drain(kv.at[x, g], kv_recv.at[g])
            for j in range(3):
                x_copy(g, j).start()

    above, below = lax.rem(z + 1, NZ), lax.rem(z + NZ - 1, NZ)

    def rs_up(i):
        chunk = lax.rem(z + NZ // 2 - i + NZ, NZ)
        return chunk, remote(part.at[chunk], up_got.at[i], rs_send.at[0, i], rs_recv.at[0, i], device(above, x, y))

    def rs_down(i):
        chunk = lax.rem(z - (NZ // 2 - 1) + i + NZ, NZ)
        return chunk, remote(part.at[chunk], down_got.at[i], rs_send.at[1, i], rs_recv.at[1, i], device(below, x, y))

    def ag_up(i):
        chunk = lax.rem(z - i + NZ, NZ)
        return remote(text_kv.at[chunk], text_kv.at[chunk], ag_send.at[0, i], ag_recv.at[0, i], device(above, x, y))

    def ag_down(i):
        chunk = lax.rem(z + i, NZ)
        return remote(text_kv.at[chunk], text_kv.at[chunk], ag_send.at[1, i], ag_recv.at[1, i], device(below, x, y))

    def rs_step(i):
        chunk, copy = rs_up(i)
        if i:
            rs_up(i - 1)[1].wait_recv()
            part[chunk] = part[chunk] + up_got[i - 1]
        copy.start()
        if i < NZ // 2 - 1:
            chunk, copy = rs_down(i)
            if i:
                rs_down(i - 1)[1].wait_recv()
                part[chunk] = part[chunk] + down_got[i - 1]
            copy.start()

    def ag_step(i):
        if i:
            ag_up(i - 1).wait_recv()
        ag_up(i).start()
        if i < NZ // 2 - 1:
            if i:
                ag_down(i - 1).wait_recv()
            ag_down(i).start()

    steps = NZ // 2
    rs_step(0)
    send_kv(0)
    to_groups(
        lambda to: cq_in.at[:, pl.ds(pl.multiple_of(to * GROUP_COLS, HEAD_DIM), GROUP_COLS)],
        cq_got.at[uly],
        cross_send.at[0],
        cross_recv.at[0],
    )
    rs_step(1)
    send_kv(1)
    rs_step(2)
    rs_step(3)
    send_q(0)
    rs_step(4)
    gather_x(0)
    rs_step(5)
    send_q(1)
    rs_step(6)
    rs_step(7)
    rs_up(steps - 1)[1].wait_recv()
    rs_down(steps - 2)[1].wait_recv()
    text_kv[z] = (part[z] + up_got[steps - 1] + down_got[steps - 2]).astype(BF16)
    ag_step(0)
    gather_x(1)
    for i in range(1, steps):
        ag_step(i)
    ag_up(steps - 1).wait_recv()
    ag_down(steps - 2).wait_recv()
    drain(cq_got, cross_recv.at[0])
    for j in range(GROUP_COLS // HEAD_DIM):
        cols = slice(j * HEAD_DIM, (j + 1) * HEAD_DIM)
        vcols = slice(GROUP_COLS + j * HEAD_DIM, GROUP_COLS + (j + 1) * HEAD_DIM)
        queries = cq_got[:, :, cols].reshape(GROUPS * ROWS, HEAD_DIM)
        keys = text_kv[:, :, cols].reshape(TEXT_ROWS, HEAD_DIM)
        values = text_kv[:, :, vcols].reshape(TEXT_ROWS, HEAD_DIM)
        result = attend(queries, [(lambda: keys, lambda: values)])
        co_stage[:, :, cols] = result.astype(BF16).reshape(GROUPS, ROWS, HEAD_DIM)
    to_groups(lambda to: co_stage.at[to], co_got.at[uly], cross_send.at[1], cross_recv.at[1])

    @pl.when(active)
    def _():
        for g in range(2):
            for j in range(3):
                x_copy(g, j).wait_recv()

        def block(step):
            at = lax.rem(x + step, NX)
            rows = 2 * SOURCES * HALF
            return (
                lambda: kv[at, :, :, 0].reshape(rows, HEAD_DIM),
                lambda: kv[at, :, :, 1].reshape(rows, HEAD_DIM),
            )

        for g in range(2):
            drain(q_got.at[g], q_recv.at[g])

            @pl.loop(0, SOURCES // TILE_SOURCES)
            def _(t):
                here = pl.ds(t * TILE_SOURCES, TILE_SOURCES)
                queries = q_got[g, here].reshape(TILE, HEAD_DIM)
                result = attend(queries, [block(step) for step in range(NX)])
                o_stage[g, here] = result.astype(BF16).reshape(TILE_SOURCES, HALF, HEAD_DIM)

                @pl.loop(0, TILE_SOURCES)
                def _(k):
                    s = t * TILE_SOURCES + k
                    target = o_got.at[my_head, pl.ds(g * HALF, HALF)]

                    @pl.when(s == me)
                    def _():
                        pltpu.make_async_copy(o_stage.at[g, s], target, o_recv.at[g]).start()

                    @pl.when(s != me)
                    def _():
                        remote(
                            o_stage.at[g, s], target, o_send.at[g], o_recv.at[g], device(s // NY, x, s % NY)
                        ).start()

    drain(co_got, cross_recv.at[1])
    for g in range(2):
        drain(o_got.at[:, pl.ds(g * HALF, HALF)], o_recv.at[g])
        rows = slice(g * HALF, (g + 1) * HALF)
        for h in range(HEADS):
            per = GROUP_COLS // HEAD_DIM
            cross = co_got[h // per, rows, (h % per) * HEAD_DIM : (h % per + 1) * HEAD_DIM]
            total = o_got[h, rows].astype(F32) + cross.astype(F32)
            out_ref[rows, h * HEAD_DIM : (h + 1) * HEAD_DIM] = total.astype(BF16)

    for i in range(steps):
        rs_up(i)[1].wait_send()
        ag_up(i).wait_send()
    for i in range(steps - 1):
        rs_down(i)[1].wait_send()
        ag_down(i).wait_send()
    drain(cq_got.at[pl.ds(0, GROUPS - 1)], cross_send.at[0])
    drain(co_got.at[pl.ds(0, GROUPS - 1)], cross_send.at[1])

    @pl.when(active)
    def _():
        for g in range(2):
            drain(kv_stage.at[g, pl.ds(0, HEADS - 1)], kv_send.at[g])
            drain(q_got.at[g, pl.ds(0, HEADS - 1)], q_send.at[g])
            drain(o_stage.at[g, pl.ds(0, SOURCES - 1)], o_send.at[g])
            for j in range(3):
                x_copy(g, j).wait_send()

    @pl.when(jnp.logical_not(active))
    def _():
        for g in range(2):
            drain(kv_stage.at[g], kv_send.at[g])
            drain(q_got.at[g, pl.ds(0, HEADS)], q_send.at[g])


def on_device(self_queries, self_keys, self_values, cross_queries, text_rows, text_projection):
    projection = text_projection.reshape(FEATURES, 2 * GROUP_COLS)
    any_space = pl.BlockSpec(memory_space=pl.ANY)
    dma = pltpu.SemaphoreType.DMA
    tokens = (ROWS, HEADS * HEAD_DIM)
    return pl.pallas_call(
        kernel,
        out_shape=jax.ShapeDtypeStruct(tokens, BF16),
        in_specs=[any_space] * 6,
        out_specs=pl.BlockSpec(memory_space=pltpu.VMEM),
        scratch_shapes=[
            pltpu.VMEM(tokens, BF16),
            pltpu.VMEM(tokens, BF16),
            pltpu.VMEM(tokens, BF16),
            pltpu.VMEM(tokens, BF16),
            pltpu.VMEM((TEXT_ROWS, FEATURES), BF16),
            pltpu.VMEM((FEATURES, 2 * GROUP_COLS), BF16),
            pltpu.VMEM((2, HEADS, 2, HALF, HEAD_DIM), BF16),
            pltpu.VMEM((NX, 2, SOURCES, 2, HALF, HEAD_DIM), BF16),
            pltpu.VMEM((2, SOURCES, HALF, HEAD_DIM), BF16),
            pltpu.VMEM((2, SOURCES, HALF, HEAD_DIM), BF16),
            pltpu.VMEM((HEADS, ROWS, HEAD_DIM), BF16),
            pltpu.VMEM((GROUPS, ROWS, GROUP_COLS), BF16),
            pltpu.VMEM((GROUPS, ROWS, GROUP_COLS), BF16),
            pltpu.VMEM((GROUPS, ROWS, GROUP_COLS), BF16),
            pltpu.VMEM((NZ, CHUNK, 2 * GROUP_COLS), F32),
            pltpu.VMEM((NZ // 2, CHUNK, 2 * GROUP_COLS), F32),
            pltpu.VMEM((NZ // 2 - 1, CHUNK, 2 * GROUP_COLS), F32),
            pltpu.VMEM((NZ, CHUNK, 2 * GROUP_COLS), BF16),
            dma((6,)),
            dma((2,)), dma((2,)),
            dma((2,)), dma((2,)),
            dma((2, 3)), dma((2, 3)),
            dma((2,)), dma((2,)),
            dma((2, NZ // 2)), dma((2, NZ // 2)),
            dma((2, NZ // 2)), dma((2, NZ // 2)),
            dma((2,)), dma((2,)),
        ],
        compiler_params=pltpu.CompilerParams(
            collective_id=0, has_side_effects=True, vmem_limit_bytes=48 * 2**20
        ),
    )(self_queries, self_keys, self_values, cross_queries, text_rows, projection)


def solution(mesh):
    tokens = P(("clip", "blk", "uly"), None)
    return jax.shard_map(
        on_device,
        mesh=mesh,
        in_specs=(tokens, tokens, tokens, tokens, P("clip", None), P("blk", None, "uly")),
        out_specs=tokens,
        check_vma=False,
    )
```
